256 devices in a mesh: hid: 32 (over x, y, z_lo), wid: 8 (over z_hi, core).
Axes of the slice: x: 4, y: 4, z: 8 (z_hi: 4, z_lo: 2; z = z_hi * 2 + z_lo), core: 2. Of those that a mesh axis runs over, the one named last changes fastest.
Arguments:
- inputs: bfloat16 [1024, 8192], P('hid', 'wid'), may hold values from -6 to 6
- out_grad: bfloat16 [1024, 8192], P('hid', 'wid'), may hold values from -6 to 6
- gate_pre: bfloat16 [1024, 28672], P('wid', 'hid'), may hold values from -8 to 8
- up_pre: bfloat16 [1024, 28672], P('wid', 'hid'), may hold values from -6 to 6
- w_gate: bfloat16 [8192, 28672], P('wid', 'hid'), may hold values from -0.0625 to 0.0625
- w_up: bfloat16 [8192, 28672], P('wid', 'hid'), may hold values from -0.0625 to 0.0625
- w_down: bfloat16 [28672, 8192], P('hid', 'wid'), may hold values from -0.03125 to 0.03125
Outputs:
- grad_inputs: bfloat16 [1024, 8192], P('hid', 'wid')
- grad_gate: bfloat16 [8192, 28672], P('wid', 'hid')
- grad_up: bfloat16 [8192, 28672], P('wid', 'hid')
- grad_down: bfloat16 [28672, 8192], P('hid', 'wid')
The draws below stay inside these ranges and needn't reach their ends.
All inputs are finite; a program needn't handle non-finite values.
Results may differ from the reference program's by a relative error of at most 0.0049.
Values may be sent and summed in bfloat16 or wider, within the bound.
No kernel may reach another device: no remote copies, remote signals or barrier semaphores. Data moves between devices by JAX's collectives and lax.ppermute only.
A program may use at most 64 MiB of HBM per device.

```python
import jax
import jax.numpy as jnp

D = 8192
FF = 28672
TOKENS = 1024


def steps_of(key, dims, split, least, top_value):
    level = 1.0
    for dim, shards_of in split:
        steps = jax.random.uniform(jax.random.fold_in(jax.random.fold_in(key, 6), dim), (shards_of,), jnp.float32, least / len(split), top_value / len(split))
        level = level * jnp.repeat(jnp.exp(steps), dims[dim] // shards_of).reshape((-1,) + (1,) * (len(dims) - 1 - dim))
    return level


def bell_draw(own_key, shape, deviation, limit, shards=(), held_as=jnp.bfloat16):
    array = deviation * jax.random.normal(own_key, shape, jnp.float32)
    if shards:
        array = array * steps_of(own_key, shape, shards, -0.22, 0.18)
    return jnp.clip(array, -limit, limit).astype(held_as)


def setup_inputs(seed: int = 0) -> dict:
    arg_keys = jax.random.split(jax.random.key(seed), 8)
    inputs = bell_draw(arg_keys[0], (TOKENS, D), 1.0, 6.0, ((0, 32), (1, 8)))
    out_grad = bell_draw(arg_keys[1], (TOKENS, D), 1.0, 6.0, ((0, 32), (1, 8)))
    gate_pre = bell_draw(arg_keys[2], (TOKENS, FF), 1.5, 8.0, ((0, 8), (1, 32)))
    up_pre = bell_draw(arg_keys[3], (TOKENS, FF), 1.0, 6.0, ((0, 8), (1, 32)))
    w_gate = bell_draw(arg_keys[4], (D, FF), D ** -0.5, 0.0625, ((0, 8), (1, 32)))
    w_up = bell_draw(arg_keys[5], (D, FF), D ** -0.5, 0.0625, ((0, 8), (1, 32)))
    w_down = bell_draw(arg_keys[6], (FF, D), FF ** -0.5, 0.03125, ((0, 32), (1, 8)))
    return dict(inputs=inputs, out_grad=out_grad, gate_pre=gate_pre, up_pre=up_pre, w_gate=w_gate, w_up=w_up, w_down=w_down)


def reference(inputs, out_grad, gate_pre, up_pre, w_gate, w_up, w_down):
    hidden_grad = jnp.dot(out_grad, w_down.T, preferred_element_type=jnp.float32)
    gate_val = gate_pre.astype(jnp.float32)
    up_val = up_pre.astype(jnp.float32)
    sig = jax.nn.sigmoid(gate_val)
    act = gate_val * sig
    hidden = (act * up_val).astype(jnp.bfloat16)
    gate_grad = (hidden_grad * up_val * sig * (1.0 + gate_val * (1.0 - sig))).astype(jnp.bfloat16)
    up_grad = (hidden_grad * act).astype(jnp.bfloat16)
    grad_down = jnp.dot(hidden.T, out_grad, preferred_element_type=jnp.float32).astype(jnp.bfloat16)
    grad_gate = jnp.dot(inputs.T, gate_grad, preferred_element_type=jnp.float32).astype(jnp.bfloat16)
    grad_up = jnp.dot(inputs.T, up_grad, preferred_element_type=jnp.float32).astype(jnp.bfloat16)
    grad_inputs = jnp.dot(gate_grad, w_gate.T, preferred_element_type=jnp.float32)
    grad_inputs = grad_inputs + jnp.dot(up_grad, w_up.T, preferred_element_type=jnp.float32)
    return grad_inputs.astype(jnp.bfloat16), grad_gate, grad_up, grad_down
```

```python
import functools

import jax
import jax.numpy as jnp
from jax import lax
from jax.experimental import pallas as pl
from jax.experimental.pallas import tpu as pltpu
from jax.sharding import PartitionSpec as P

BF = jnp.bfloat16
F32 = jnp.float32
T, DB, FB = 1024, 1024, 896
HALF = 512
COL_TILES = ((0, 256), (256, 256), (512, 256), (768, 128))
VMEM = pl.BlockSpec(memory_space=pltpu.VMEM)
SMEM = pl.BlockSpec(memory_space=pltpu.SMEM)


def shift_x(value, step):
    return lax.ppermute(value, "hid", [(h, (h + 8 * step) % 32) for h in range(32)])


def shift_y(value, step):
    return lax.ppermute(
        value, "hid", [(h, h // 8 * 8 + (h % 8 + 2 * step) % 8) for h in range(32)]
    )


def swap_zl(value):
    return lax.ppermute(value, "hid", [(h, h ^ 1) for h in range(32)])


def shift_zh(value, step):
    return lax.ppermute(value, "wid", [(w, (w + 2 * step) % 8) for w in range(8)])


def swap_core(value):
    return lax.ppermute(value, "wid", [(w, w ^ 1) for w in range(8)])


def local_row(pos, bx, by):
    zh, core = pos[3], pos[4]
    return pl.multiple_of(
        ((by // 2) ^ core) * 512 + ((bx - zh) & 3) * 128 + (by & 1) * 64, 64
    )


def assemble(pos, first, second, out):
    x, y = pos[0], pos[1]
    for k in range(4):
        for j in range(4):
            row = local_row(pos, (x - k) & 3, (y - j) & 3)
            out[pl.ds(row, 64), :HALF] = first[j][k * 64 : (k + 1) * 64, :]
            out[pl.ds(row, 64), HALF:] = second[k][j * 64 : (j + 1) * 64, :]


def dot_nt(left, right):
    return lax.dot_general(left, right, (((1,), (1,)), ((), ())), preferred_element_type=F32)


def dot_tn(left, right):
    return lax.dot_general(left, right, (((0,), (0,)), ((), ())), preferred_element_type=F32)


def gather_rows(shard, zl):
    other = swap_zl(shard)
    pair = jnp.where(
        zl == 0, jnp.concatenate([shard, other]), jnp.concatenate([other, shard])
    )
    left, right = pair[:, :HALF], pair[:, HALF:]
    lefts = [left] + [shift_x(left, k) for k in (1, 2, 3)]
    rights = [right] + [shift_y(right, k) for k in (1, 2, 3)]
    left, right = jnp.concatenate(lefts), jnp.concatenate(rights)
    first = [left] + [shift_y(left, k) for k in (1, 2, 3)]
    second = [right] + [shift_x(right, k) for k in (1, 2, 3)]
    return first + second


def call(kernel, outs, cost, scratch=()):
    flops, nbytes = cost
    return lambda *args: pl.pallas_call(
        kernel,
        out_shape=[jax.ShapeDtypeStruct(s, d) for s, d in outs],
        in_specs=[SMEM] + [VMEM] * (len(args) - 1),
        out_specs=[VMEM] * len(outs),
        scratch_shapes=list(scratch),
        cost_estimate=pl.CostEstimate(flops=flops, bytes_accessed=nbytes, transcendentals=0),
        compiler_params=pltpu.CompilerParams(vmem_limit_bytes=50 * 2**20),
    )(*args)


def hidden_grad_kernel(pos, *refs):
    pieces, w_down, grads, keep, send = refs[:8], refs[8], refs[9], refs[10], refs[11]
    assemble(pos, pieces[:4], pieces[4:], grads)
    for start, width in COL_TILES:
        cols = slice(start, start + width)
        part = dot_nt(grads[...], w_down[cols, :])
        keep[:, cols] = part[:512]
        send[:, cols] = part[512:].astype(BF)


def pair_sum_kernel(pos, keep, got, own, one, two, three):
    own[...] = keep[:128] + got[:128].astype(F32)
    for k, out in enumerate((one, two, three)):
        rows = slice(128 * (k + 1), 128 * (k + 2))
        out[...] = (keep[rows] + got[rows].astype(F32)).astype(BF)


def ring_sum_kernel(pos, own, one, two, three, out):
    total = own[...] + one[...].astype(F32) + two[...].astype(F32) + three[...].astype(F32)
    out[...] = total.astype(BF)


def down_kernel(pos, *refs):
    acts, grads, out, hidden = refs[:8], refs[8], refs[9], refs[10]
    for i in range(8):
        gate = acts[i][:128].astype(F32)
        up = acts[i][128:].astype(F32)
        sig = jax.nn.sigmoid(gate)
        hidden[i * 128 : (i + 1) * 128] = (gate * sig * up).astype(BF)
    for start in range(0, DB, 256):
        cols = slice(start, start + 256)
        out[:, cols] = dot_tn(hidden[...], grads[:, cols]).astype(BF)


def input_grad_kernel(pos, *refs):
    acts, hgs = refs[:8], refs[8:16]
    w_gate, w_up, out, gate_grad, up_grad = refs[16:]
    for i in range(8):
        rows = slice(i * 128, (i + 1) * 128)
        gate = acts[i][:128].astype(F32)
        up = acts[i][128:].astype(F32)
        hg = hgs[i][...].astype(F32)
        sig = jax.nn.sigmoid(gate)
        gate_grad[rows] = (hg * up * sig * (1.0 + gate * (1.0 - sig))).astype(BF)
        up_grad[rows] = (hg * (gate * sig)).astype(BF)
    zh, core = pos[3], pos[4]
    for start in range(0, DB, 256):
        cols = slice(start, start + 256)
        part = dot_nt(gate_grad[...], w_gate[cols, :]) + dot_nt(up_grad[...], w_up[cols, :])
        part = part.astype(BF)
        for i in range(8):
            bx = (zh + i % 4) & 3
            by = 2 * ((i // 4) ^ core)
            row = pl.multiple_of(bx * 256 + by * 64, 128)
            out[pl.ds(row, 128), cols] = part[i * 128 : (i + 1) * 128]


def weight_grad_kernel(pos, *refs):
    pieces, gate_grad, up_grad, out_gate, out_up, inputs = refs[:8], *refs[8:]
    assemble(pos, pieces[:4], pieces[4:], inputs)
    for start, width in COL_TILES:
        cols = slice(start, start + width)
        out_gate[:, cols] = dot_tn(inputs[...], gate_grad[:, cols]).astype(BF)
        out_up[:, cols] = dot_tn(inputs[...], up_grad[:, cols]).astype(BF)


MM = 2 * T * DB * FB
MB = 2**20


def spread_core(mine):
    return list(mine) + [swap_core(p) for p in mine]


def gather_zh(block):
    got = [shift_zh(block, k) for k in (1, 2, 3)]
    return [block, got[2], got[1], got[0]]


def per_device(inputs, out_grad, gate_pre, up_pre, w_gate, w_up, w_down):
    h, w = lax.axis_index("hid"), lax.axis_index("wid")
    zl = h % 2
    pos = jnp.stack([h // 8, h // 2 % 4, zl, w // 2, w % 2]).astype(jnp.int32)

    acts = spread_core(gather_zh(jnp.concatenate([gate_pre, up_pre])))
    grad_pieces = gather_rows(out_grad, zl)
    input_pieces = gather_rows(inputs, zl)

    all_grads, keep, send = call(
        hidden_grad_kernel,
        [((T, DB), BF), ((512, FB), F32), ((512, FB), BF)],
        (MM, 10 * MB),
    )(pos, *grad_pieces, w_down)
    got = swap_core(send)
    own, one, two, three = call(
        pair_sum_kernel,
        [((128, FB), F32)] + [((128, FB), BF)] * 3,
        (FB * 512, 4 * MB),
    )(pos, keep, got)
    got = [shift_zh(one, 1), shift_zh(two, 2), shift_zh(three, 3)]
    (hg,) = call(ring_sum_kernel, [((128, FB), BF)], (FB * 512, MB))(pos, own, *got)
    hgs = spread_core(gather_zh(hg))

    (grad_down,) = call(
        down_kernel, [((FB, DB), BF)], (MM, 8 * MB), [pltpu.VMEM((T, FB), BF)]
    )(pos, *acts, all_grads)

    partial, gate_grad, up_grad = call(
        input_grad_kernel,
        [((T, DB), BF), ((T, FB), BF), ((T, FB), BF)],
        (2 * MM, 15 * MB),
    )(pos, *acts, *hgs, w_gate, w_up)
    parts = lax.all_to_all(partial, "hid", split_axis=0, concat_axis=0, tiled=True)
    grad_inputs = jnp.sum(parts.reshape(32, 32, DB).astype(F32), axis=0).astype(BF)
    grad_gate, grad_up = call(
        weight_grad_kernel,
        [((DB, FB), BF), ((DB, FB), BF)],
        (2 * MM, 10 * MB),
        [pltpu.VMEM((T, DB), BF)],
    )(pos, *input_pieces, gate_grad, up_grad)
    return (grad_inputs, grad_gate, grad_up, grad_down)


def solution(mesh):
    in_specs = (
        P("hid", "wid"),
        P("hid", "wid"),
        P("wid", "hid"),
        P("wid", "hid"),
        P("wid", "hid"),
        P("wid", "hid"),
        P("hid", "wid"),
    )
    out_specs = (P("hid", "wid"), P("wid", "hid"), P("wid", "hid"), P("hid", "wid"))
    return jax.shard_map(
        per_device, mesh=mesh, in_specs=in_specs, out_specs=out_specs, check_vma=False
    )
```

```python
import functools

import jax
import jax.numpy as jnp
from jax import lax
from jax.experimental import pallas as pl
from jax.experimental.pallas import tpu as pltpu
from jax.sharding import PartitionSpec as P

BF = jnp.bfloat16
F32 = jnp.float32
T, DB, FB = 1024, 1024, 896
COL_TILES = ((0, 256), (256, 256), (512, 256), (768, 128))
VMEM = pl.BlockSpec(memory_space=pltpu.VMEM)
ANY = pl.BlockSpec(memory_space=pl.ANY)
HBM = pl.BlockSpec(memory_space=pltpu.HBM)
SMEM = pl.BlockSpec(memory_space=pltpu.SMEM)


def shift_x(value, step):
    return lax.ppermute(value, "hid", [(h, (h + 8 * step) % 32) for h in range(32)])


def shift_y(value, step):
    return lax.ppermute(
        value, "hid", [(h, h // 8 * 8 + (h % 8 + 2 * step) % 8) for h in range(32)]
    )


def swap_x(value, bit):
    return lax.ppermute(value, "hid", [(h, h ^ (8 * bit)) for h in range(32)])


def swap_y(value, bit):
    return lax.ppermute(value, "hid", [(h, h ^ (2 * bit)) for h in range(32)])


def swap_zl(value):
    return lax.ppermute(value, "hid", [(h, h ^ 1) for h in range(32)])


def shift_zh(value, step):
    return lax.ppermute(value, "wid", [(w, (w + 2 * step) % 8) for w in range(8)])


def swap_core(value):
    return lax.ppermute(value, "wid", [(w, w ^ 1) for w in range(8)])


def local_row(pos, bx, by):
    zh, core = pos[3], pos[4]
    return pl.multiple_of(
        ((by // 2) ^ core) * 512 + ((bx - zh) & 3) * 128 + (by & 1) * 64, 64
    )


def to_local(pos, rows, out, place):
    for i in range(rows.shape[0] // 64):
        out[pl.ds(local_row(pos, *place(i)), 64)] = rows[i * 64 : (i + 1) * 64]


def dot_nt(left, right):
    return lax.dot_general(left, right, (((1,), (1,)), ((), ())), preferred_element_type=F32)


def dot_tn(left, right):
    return lax.dot_general(left, right, (((0,), (0,)), ((), ())), preferred_element_type=F32)


def call(kernel, outs, cost, scratch=(), whole=0, after=0, stay=0):
    flops, nbytes = cost

    def body(*refs):
        n = len(refs) - len(outs) - len(scratch)
        kernel(*refs[: n - after], *refs[n:])

    def run(*args):
        plain = len(args) - whole - after
        kept = [
            pltpu.with_memory_space_constraint(arg, pltpu.HBM)
            for arg in args[plain : plain + whole + stay]
        ]
        return pl.pallas_call(
            body,
            out_shape=[(pltpu.HBM if o[2:] else jax.ShapeDtypeStruct)(*o[:2]) for o in outs],
            in_specs=[SMEM] + [VMEM] * (plain - 1) + [HBM] * (whole + stay) + [ANY] * (after - stay),
            out_specs=[HBM if o[2:] else VMEM for o in outs],
            scratch_shapes=list(scratch),
            cost_estimate=pl.CostEstimate(flops=flops, bytes_accessed=nbytes, transcendentals=0),
            compiler_params=pltpu.CompilerParams(vmem_limit_bytes=16 * 2**20),
        )(*args[:plain], *kept, *args[plain + whole + stay :])

    return run


def start_all(copies):
    for copy in copies:
        copy.start()
    return copies


def wait_all(copies):
    for copy in copies:
        copy.wait()


def pair_kernel(pos, other, rows_other, mine, rows_mine, gate, up, out, rows_out, acts_out, sems):
    row = pl.multiple_of(pos[2] * 32, 32)
    other_row = pl.multiple_of(32 - pos[2] * 32, 32)
    moves = [
        (mine, out.at[pl.ds(row, 32)]),
        (other, out.at[pl.ds(other_row, 32)]),
        (rows_mine, rows_out.at[pl.ds(row, 32)]),
        (rows_other, rows_out.at[pl.ds(other_row, 32)]),
        (gate, acts_out.at[pl.ds(0, 128)]),
        (up, acts_out.at[pl.ds(128, 128)]),
    ]
    wait_all(
        start_all([pltpu.make_async_copy(a, b, sems.at[i]) for i, (a, b) in enumerate(moves)])
    )


def rows_kernel(pos, *refs):
    for i, part in enumerate(refs[:4]):
        refs[4][i * 64 : (i + 1) * 64] = part[...]


def hidden_grad_kernel(pos, *refs):
    pieces, (w_down, near, far, grads, keep, send, rows_out) = refs[:4], refs[4:]
    for j, piece in enumerate(pieces):
        to_local(pos, piece, grads, lambda k, j=j: ((pos[0] - k) & 3, (pos[1] - j) & 3))
    for start, width in COL_TILES:
        cols = slice(start, start + width)
        part = dot_nt(grads[...], w_down[cols, :])
        keep[:, cols] = part[:512]
        send[:, cols] = part[512:]
    rows_out[:128] = near[...]
    rows_out[128:] = far[...]


def pair_sum_kernel(pos, keep, got, *refs):
    acts = refs[:5]
    own, one, two, three, acts_out, sems = refs[5:]
    copies = []
    for i, (block, row) in enumerate(zip(acts, (0, 256, 768, 512, 640))):
        place = acts_out.at[pl.ds(row, block.shape[0])]
        copies.append(pltpu.make_async_copy(block, place, sems.at[i]))
    start_all(copies)
    own[...] = keep[:128] + got[:128]
    for k, out in enumerate((one, two, three)):
        rows = slice(128 * (k + 1), 128 * (k + 2))
        out[...] = (keep[rows] + got[rows]).astype(BF)
    wait_all(copies)


def ring_sum_kernel(pos, own, one, two, three, near, far, out, rows_out):
    rows_out[:256] = near[...]
    rows_out[256:] = far[...]
    total = own[...] + one[...].astype(F32) + two[...].astype(F32) + three[...].astype(F32)
    out[...] = total.astype(BF)


def down_kernel(pos, *refs):
    blocks, (grads, out, act_out, slope_out, hidden) = refs[:2], refs[2:]
    for i in range(8):
        rows = slice(i * 128, (i + 1) * 128)
        start = 256 * (i % 4)
        gate = blocks[i // 4][start : start + 128].astype(F32)
        up = blocks[i // 4][start + 128 : start + 256].astype(F32)
        sig = jax.nn.sigmoid(gate)
        act = gate * sig
        act_out[rows] = act
        slope_out[rows] = up * sig * (1.0 + gate * (1.0 - sig))
        hidden[rows] = (act * up).astype(BF)
    for start in range(0, DB, 256):
        cols = slice(start, start + 256)
        out[:, cols] = dot_tn(hidden[...], grads[:, cols]).astype(BF)


def sum_kernel(pos, parts, out):
    total = parts[0].astype(F32)
    for i in range(1, 32):
        total = total + parts[i].astype(F32)
    out[...] = total.astype(BF)


def input_grad_kernel(pos, *refs):
    hgs, (act, slope, w_gate, w_up, out, gate_out, up_out) = refs[:8], refs[8:15]
    gate_grad, up_grad, part, sems = refs[15:]
    for i in range(8):
        rows = slice(i * 128, (i + 1) * 128)
        hg = hgs[i][...].astype(F32)
        gate_grad[rows] = (hg * slope[rows]).astype(BF)
        up_grad[rows] = (hg * act[rows]).astype(BF)
    copies = start_all(
        [
            pltpu.make_async_copy(gate_grad, gate_out, sems.at[4]),
            pltpu.make_async_copy(up_grad, up_out, sems.at[5]),
        ]
    )
    zh, core = pos[3], pos[4]
    for n, start in enumerate(range(0, DB, 256)):
        cols = slice(start, start + 256)
        block = dot_nt(gate_grad[...], w_gate[cols, :]) + dot_nt(up_grad[...], w_up[cols, :])
        block = block.astype(BF)
        for i in range(8):
            bx = (zh + i % 4) & 3
            by = 2 * ((i // 4) ^ core)
            row = pl.multiple_of(bx * 256 + by * 64, 128)
            part[n, pl.ds(row, 128)] = block[i * 128 : (i + 1) * 128]
        copies += start_all([pltpu.make_async_copy(part.at[n], out.at[:, cols], sems.at[n])])
    wait_all(copies)


def weight_grad_kernel(pos, *refs):
    near, far, gate_grad, up_grad, out_gate, out_up, inputs = refs
    for first, rows in ((0, near), (8, far)):

        def place(i, first=first):
            i += first
            return (i >> 1 & 1 | i >> 2 & 2) ^ pos[0], (i & 1 | i >> 1 & 2) ^ pos[1]

        to_local(pos, rows, inputs, place)
    for start, width in COL_TILES:
        cols = slice(start, start + width)
        out_gate[:, cols] = dot_tn(inputs[...], gate_grad[:, cols]).astype(BF)
        out_up[:, cols] = dot_tn(inputs[...], up_grad[:, cols]).astype(BF)


MM = 2 * T * DB * FB
MB = 2**20
LONG = (12 * MM, 80 * MB)
SHORT = (0, 0)


def spread_core(mine):
    return list(mine) + [swap_core(p) for p in mine]


def gather_zh(block):
    got = [shift_zh(block, k) for k in (1, 2, 3)]
    return [block, got[2], got[1], got[0]]


def ring_zh(block):
    above, below = shift_zh(block, 1), shift_zh(block, 3)
    return [block, below, above, shift_zh(above[:128], 1), shift_zh(below[128:], 3)]


def per_device(inputs, out_grad, gate_pre, up_pre, w_gate, w_up, w_down):
    h, w = lax.axis_index("hid"), lax.axis_index("wid")
    pos = jnp.stack([h // 8, h // 2 % 4, h % 2, w // 2, w % 2]).astype(jnp.int32)

    block, near, acts = call(
        pair_kernel,
        [((64, DB), BF), ((64, DB), BF), ((256, FB), BF)],
        SHORT,
        [pltpu.SemaphoreType.DMA((6,))],
        whole=4,
    )(pos, swap_zl(out_grad), swap_zl(inputs), out_grad, inputs, gate_pre, up_pre)
    acts = ring_zh(acts)
    (block,) = call(rows_kernel, [((256, DB), BF)], (0, MB))(
        pos, block, *[shift_x(block, k) for k in (1, 2, 3)]
    )
    near = jnp.concatenate([near, swap_y(near, 1)])
    far = swap_x(near, 1)
    all_grads, keep, send, near = call(
        hidden_grad_kernel,
        [((T, DB), BF), ((512, FB), F32), ((512, FB), F32), ((256, DB), BF)],
        LONG,
        after=2,
    )(pos, block, *[shift_y(block, k) for k in (1, 2, 3)], w_down, near, far, *acts[3:])
    far = swap_y(near, 2)
    own, one, two, three, acts = call(
        pair_sum_kernel,
        [((128, FB), F32)] + [((128, FB), BF)] * 3 + [((T, FB), BF)],
        LONG,
        [pltpu.SemaphoreType.DMA((5,))],
        whole=5,
    )(pos, keep, swap_core(send), *acts)
    got = [shift_zh(one, 1), shift_zh(two, 2), shift_zh(three, 3)]
    grad_down, act, slope = call(
        down_kernel,
        [((FB, DB), BF), ((T, FB), F32), ((T, FB), F32)],
        (MM, 16 * MB),
        [pltpu.VMEM((T, FB), BF)],
    )(pos, acts, swap_core(acts), all_grads)
    hg, near = call(
        ring_sum_kernel, [((128, FB), BF), ((512, DB), BF)], LONG, after=1
    )(pos, own, *got, near, far, act)
    far = swap_x(near, 2)
    hgs = spread_core(gather_zh(hg))
    partial, gate_grad, up_grad = call(
        input_grad_kernel,
        [((T, DB), BF, HBM), ((T, FB), BF, HBM), ((T, FB), BF, HBM)],
        (2 * MM, 15 * MB),
        [
            pltpu.VMEM((T, FB), BF),
            pltpu.VMEM((T, FB), BF),
            pltpu.VMEM((4, T, 256), BF),
            pltpu.SemaphoreType.DMA((6,)),
        ],
        after=1,
    )(pos, *hgs, act, slope, w_gate, w_up, far)
    parts = lax.all_to_all(partial, "hid", split_axis=0, concat_axis=0, tiled=True)
    (grad_inputs,) = call(sum_kernel, [((32, DB), BF)], (MB, 2 * MB))(
        pos, parts.reshape(32, 32, DB)
    )
    grad_gate, grad_up = call(
        weight_grad_kernel,
        [((DB, FB), BF), ((DB, FB), BF)],
        (2 * MM, 10 * MB),
        [pltpu.VMEM((T, DB), BF)],
    )(pos, near, far, gate_grad, up_grad)
    return (grad_inputs, grad_gate, grad_up, grad_down)


def solution(mesh):
    in_specs = (
        P("hid", "wid"),
        P("hid", "wid"),
        P("wid", "hid"),
        P("wid", "hid"),
        P("wid", "hid"),
        P("wid", "hid"),
        P("hid", "wid"),
    )
    out_specs = (P("hid", "wid"), P("wid", "hid"), P("wid", "hid"), P("hid", "wid"))
    return jax.shard_map(
        per_device, mesh=mesh, in_specs=in_specs, out_specs=out_specs, check_vma=False
    )
```

```python
import functools

import jax
import jax.numpy as jnp
from jax import lax
from jax.experimental import pallas as pl
from jax.experimental.pallas import tpu as pltpu
from jax.sharding import PartitionSpec as P

BF = jnp.bfloat16
F32 = jnp.float32
T, DB, FB = 1024, 1024, 896
COL_TILES = ((0, 256), (256, 256), (512, 256), (768, 128))
VMEM = pl.BlockSpec(memory_space=pltpu.VMEM)
ANY = pl.BlockSpec(memory_space=pl.ANY)
HBM = pl.BlockSpec(memory_space=pltpu.HBM)
SMEM = pl.BlockSpec(memory_space=pltpu.SMEM)


def shift_x(value, step):
    return lax.ppermute(value, "hid", [(h, (h + 8 * step) % 32) for h in range(32)])


def shift_y(value, step):
    return lax.ppermute(
        value, "hid", [(h, h // 8 * 8 + (h % 8 + 2 * step) % 8) for h in range(32)]
    )


def swap_x(value, bit):
    return lax.ppermute(value, "hid", [(h, h ^ (8 * bit)) for h in range(32)])


def swap_y(value, bit):
    return lax.ppermute(value, "hid", [(h, h ^ (2 * bit)) for h in range(32)])


def swap_zl(value):
    return lax.ppermute(value, "hid", [(h, h ^ 1) for h in range(32)])


def shift_zh(value, step):
    return lax.ppermute(value, "wid", [(w, (w + 2 * step) % 8) for w in range(8)])


def swap_core(value):
    return lax.ppermute(value, "wid", [(w, w ^ 1) for w in range(8)])


def local_row(pos, bx, by):
    zh, core = pos[3], pos[4]
    return pl.multiple_of(
        ((by // 2) ^ core) * 512 + ((bx - zh) & 3) * 128 + (by & 1) * 64, 64
    )


def to_local(pos, rows, out, place):
    for i in range(rows.shape[0] // 64):
        out[pl.ds(local_row(pos, *place(i)), 64)] = rows[i * 64 : (i + 1) * 64]


def dot_nt(left, right):
    return lax.dot_general(left, right, (((1,), (1,)), ((), ())), preferred_element_type=F32)


def dot_tn(left, right):
    return lax.dot_general(left, right, (((0,), (0,)), ((), ())), preferred_element_type=F32)


def call(kernel, outs, cost, scratch=(), whole=0, after=0, stay=0):
    flops, nbytes = cost

    def body(*refs):
        n = len(refs) - len(outs) - len(scratch)
        kernel(*refs[: n - after], *refs[n:])

    def run(*args):
        plain = len(args) - whole - after
        kept = [
            pltpu.with_memory_space_constraint(arg, pltpu.HBM)
            for arg in args[plain : plain + whole + stay]
        ]
        return pl.pallas_call(
            body,
            out_shape=[(pltpu.HBM if o[2:] else jax.ShapeDtypeStruct)(*o[:2]) for o in outs],
            in_specs=[SMEM] + [VMEM] * (plain - 1) + [HBM] * (whole + stay) + [ANY] * (after - stay),
            out_specs=[HBM if o[2:] else VMEM for o in outs],
            scratch_shapes=list(scratch),
            cost_estimate=pl.CostEstimate(flops=flops, bytes_accessed=nbytes, transcendentals=0),
            compiler_params=pltpu.CompilerParams(vmem_limit_bytes=16 * 2**20),
        )(*args[:plain], *kept, *args[plain + whole + stay :])

    return run


def start_all(copies):
    for copy in copies:
        copy.start()
    return copies


def wait_all(copies):
    for copy in copies:
        copy.wait()


def pair_kernel(pos, other, rows_other, mine, rows_mine, gate, up, out, rows_out, acts_out, sems):
    row = pl.multiple_of(pos[2] * 32, 32)
    other_row = pl.multiple_of(32 - pos[2] * 32, 32)
    moves = [
        (mine, out.at[pl.ds(row, 32)]),
        (other, out.at[pl.ds(other_row, 32)]),
        (rows_mine, rows_out.at[pl.ds(row, 32)]),
        (rows_other, rows_out.at[pl.ds(other_row, 32)]),
        (gate, acts_out.at[pl.ds(0, 128)]),
        (up, acts_out.at[pl.ds(128, 128)]),
    ]
    wait_all(
        start_all([pltpu.make_async_copy(a, b, sems.at[i]) for i, (a, b) in enumerate(moves)])
    )


def rows_kernel(pos, *refs):
    for i, part in enumerate(refs[:4]):
        refs[4][i * 64 : (i + 1) * 64] = part[...]


def hidden_grad_kernel(pos, *refs):
    pieces, (w_down, near, far, grads, keep, send, rows_out) = refs[:4], refs[4:]
    for j, piece in enumerate(pieces):
        to_local(pos, piece, grads, lambda k, j=j: ((pos[0] - k) & 3, (pos[1] - j) & 3))
    for start, width in COL_TILES:
        cols = slice(start, start + width)
        part = dot_nt(grads[...], w_down[cols, :])
        keep[:, cols] = part[:512]
        send[:, cols] = part[512:]
    rows_out[:128] = near[...]
    rows_out[128:] = far[...]


def acts_kernel(pos, here, below, above, far_gate, far_up, out):
    row = 0
    for block in (here, below, far_gate, far_up, above):
        rows = block.shape[0]
        out[row : row + rows] = block[...]
        row += rows


def pair_sum_kernel(pos, keep, got, own, one, two, three):
    own[...] = keep[:128] + got[:128]
    for k, out in enumerate((one, two, three)):
        rows = slice(128 * (k + 1), 128 * (k + 2))
        out[...] = (keep[rows] + got[rows]).astype(BF)


def ring_sum_kernel(pos, own, one, two, three, out):
    total = own[...] + one[...].astype(F32) + two[...].astype(F32) + three[...].astype(F32)
    out[...] = total.astype(BF)


def down_kernel(pos, *refs):
    blocks, near, far, grads, out, act_out, slope_out, rows_out, hidden = refs[:2], *refs[2:]
    rows_out[:256] = near[...]
    rows_out[256:] = far[...]
    for i in range(8):
        rows = slice(i * 128, (i + 1) * 128)
        start = 256 * (i % 4)
        gate = blocks[i // 4][start : start + 128].astype(F32)
        up = blocks[i // 4][start + 128 : start + 256].astype(F32)
        sig = jax.nn.sigmoid(gate)
        act = gate * sig
        act_out[rows] = act
        slope_out[rows] = up * sig * (1.0 + gate * (1.0 - sig))
        hidden[rows] = (act * up).astype(BF)
    for start in range(0, DB, 256):
        cols = slice(start, start + 256)
        out[:, cols] = dot_tn(hidden[...], grads[:, cols]).astype(BF)


def sum_kernel(pos, parts, out):
    total = parts[0].astype(F32)
    for i in range(1, 32):
        total = total + parts[i].astype(F32)
    out[...] = total.astype(BF)


def input_grad_kernel(pos, *refs):
    hgs, (act, slope, w_gate, w_up, out, gate_out, up_out) = refs[:8], refs[8:15]
    gate_grad, up_grad, part, sems = refs[15:]
    for i in range(8):
        rows = slice(i * 128, (i + 1) * 128)
        hg = hgs[i][...].astype(F32)
        gate_grad[rows] = (hg * slope[rows]).astype(BF)
        up_grad[rows] = (hg * act[rows]).astype(BF)
    copies = start_all(
        [
            pltpu.make_async_copy(gate_grad, gate_out, sems.at[4]),
            pltpu.make_async_copy(up_grad, up_out, sems.at[5]),
        ]
    )
    zh, core = pos[3], pos[4]
    for n, start in enumerate(range(0, DB, 256)):
        cols = slice(start, start + 256)
        block = dot_nt(gate_grad[...], w_gate[cols, :]) + dot_nt(up_grad[...], w_up[cols, :])
        block = block.astype(BF)
        for i in range(8):
            bx = (zh + i % 4) & 3
            by = 2 * ((i // 4) ^ core)
            row = pl.multiple_of(bx * 256 + by * 64, 128)
            part[n, pl.ds(row, 128)] = block[i * 128 : (i + 1) * 128]
        copies += start_all([pltpu.make_async_copy(part.at[n], out.at[:, cols], sems.at[n])])
    wait_all(copies)


def weight_grad_kernel(pos, *refs):
    near, far, gate_grad, up_grad, out_gate, out_up, inputs = refs
    for first, rows in ((0, near), (8, far)):

        def place(i, first=first):
            i += first
            return (i >> 1 & 1 | i >> 2 & 2) ^ pos[0], (i & 1 | i >> 1 & 2) ^ pos[1]

        to_local(pos, rows, inputs, place)
    for start, width in COL_TILES:
        cols = slice(start, start + width)
        out_gate[:, cols] = dot_tn(inputs[...], gate_grad[:, cols]).astype(BF)
        out_up[:, cols] = dot_tn(inputs[...], up_grad[:, cols]).astype(BF)


MM = 2 * T * DB * FB
MB = 2**20
LONG = (12 * MM, 80 * MB)
SHORT = (0, 0)


def spread_core(mine):
    return list(mine) + [swap_core(p) for p in mine]


def gather_zh(block):
    got = [shift_zh(block, k) for k in (1, 2, 3)]
    return [block, got[2], got[1], got[0]]


def ring_zh(block):
    above, below = shift_zh(block, 1), shift_zh(block, 3)
    return [block, below, above, shift_zh(above[:128], 1), shift_zh(below[128:], 3)]


def per_device(inputs, out_grad, gate_pre, up_pre, w_gate, w_up, w_down):
    h, w = lax.axis_index("hid"), lax.axis_index("wid")
    pos = jnp.stack([h // 8, h // 2 % 4, h % 2, w // 2, w % 2]).astype(jnp.int32)

    block, near, acts = call(
        pair_kernel,
        [((64, DB), BF), ((64, DB), BF), ((256, FB), BF)],
        SHORT,
        [pltpu.SemaphoreType.DMA((6,))],
        whole=4,
    )(pos, swap_zl(out_grad), swap_zl(inputs), out_grad, inputs, gate_pre, up_pre)
    acts = ring_zh(acts)
    (block,) = call(rows_kernel, [((256, DB), BF)], (0, MB))(
        pos, block, *[shift_x(block, k) for k in (1, 2, 3)]
    )
    near = jnp.concatenate([near, swap_y(near, 1)])
    far = swap_x(near, 1)
    all_grads, keep, send, near = call(
        hidden_grad_kernel,
        [((T, DB), BF), ((512, FB), F32), ((512, FB), F32), ((256, DB), BF)],
        LONG,
        after=2,
    )(pos, block, *[shift_y(block, k) for k in (1, 2, 3)], w_down, near, far, *acts[3:])
    far = swap_y(near, 2)
    (acts,) = call(acts_kernel, [((T, FB), BF)], SHORT, after=1)(pos, *acts, near)
    own, one, two, three = call(
        pair_sum_kernel, [((128, FB), F32)] + [((128, FB), BF)] * 3, LONG
    )(pos, keep, swap_core(send))
    got = [shift_zh(one, 1), shift_zh(two, 2), shift_zh(three, 3)]
    grad_down, act, slope, near = call(
        down_kernel,
        [((FB, DB), BF), ((T, FB), F32), ((T, FB), F32), ((512, DB), BF)],
        (MM, 16 * MB),
        [pltpu.VMEM((T, FB), BF)],
    )(pos, acts, swap_core(acts), near, far, all_grads)
    far = swap_x(near, 2)
    (hg,) = call(ring_sum_kernel, [((128, FB), BF)], LONG, after=1)(pos, own, *got, act)
    hgs = spread_core(gather_zh(hg))
    partial, gate_grad, up_grad = call(
        input_grad_kernel,
        [((T, DB), BF, HBM), ((T, FB), BF, HBM), ((T, FB), BF, HBM)],
        (2 * MM, 15 * MB),
        [
            pltpu.VMEM((T, FB), BF),
            pltpu.VMEM((T, FB), BF),
            pltpu.VMEM((4, T, 256), BF),
            pltpu.SemaphoreType.DMA((6,)),
        ],
        after=1,
    )(pos, *hgs, act, slope, w_gate, w_up, far)
    parts = lax.all_to_all(partial, "hid", split_axis=0, concat_axis=0, tiled=True)
    (grad_inputs,) = call(sum_kernel, [((32, DB), BF)], (MB, 2 * MB))(
        pos, parts.reshape(32, 32, DB)
    )
    grad_gate, grad_up = call(
        weight_grad_kernel,
        [((DB, FB), BF), ((DB, FB), BF)],
        (2 * MM, 10 * MB),
        [pltpu.VMEM((T, DB), BF)],
    )(pos, near, far, gate_grad, up_grad)
    return (grad_inputs, grad_gate, grad_up, grad_down)


def solution(mesh):
    in_specs = (
        P("hid", "wid"),
        P("hid", "wid"),
        P("wid", "hid"),
        P("wid", "hid"),
        P("wid", "hid"),
        P("wid", "hid"),
        P("hid", "wid"),
    )
    out_specs = (P("hid", "wid"), P("wid", "hid"), P("wid", "hid"), P("hid", "wid"))
    return jax.shard_map(
        per_device, mesh=mesh, in_specs=in_specs, out_specs=out_specs, check_vma=False
    )
```

```python
import functools

import jax
import jax.numpy as jnp
from jax import lax
from jax.experimental import pallas as pl
from jax.experimental.pallas import tpu as pltpu
from jax.sharding import PartitionSpec as P

BF = jnp.bfloat16
F32 = jnp.float32
T, DB, FB = 1024, 1024, 896
COL_TILES = ((0, 256), (256, 256), (512, 256), (768, 128))
VMEM = pl.BlockSpec(memory_space=pltpu.VMEM)
ANY = pl.BlockSpec(memory_space=pl.ANY)
HBM = pl.BlockSpec(memory_space=pltpu.HBM)
SMEM = pl.BlockSpec(memory_space=pltpu.SMEM)


def shift_x(value, step):
    return lax.ppermute(value, "hid", [(h, (h + 8 * step) % 32) for h in range(32)])


def shift_y(value, step):
    return lax.ppermute(
        value, "hid", [(h, h // 8 * 8 + (h % 8 + 2 * step) % 8) for h in range(32)]
    )


def swap_x(value, bit):
    return lax.ppermute(value, "hid", [(h, h ^ (8 * bit)) for h in range(32)])


def swap_y(value, bit):
    return lax.ppermute(value, "hid", [(h, h ^ (2 * bit)) for h in range(32)])


def swap_zl(value):
    return lax.ppermute(value, "hid", [(h, h ^ 1) for h in range(32)])


def shift_zh(value, step):
    return lax.ppermute(value, "wid", [(w, (w + 2 * step) % 8) for w in range(8)])


def swap_core(value):
    return lax.ppermute(value, "wid", [(w, w ^ 1) for w in range(8)])


def local_row(pos, bx, by):
    zh, core = pos[3], pos[4]
    return pl.multiple_of(
        ((by // 2) ^ core) * 512 + ((bx - zh) & 3) * 128 + (by & 1) * 64, 64
    )


def to_local(pos, rows, out, place):
    for i in range(rows.shape[0] // 64):
        out[pl.ds(local_row(pos, *place(i)), 64)] = rows[i * 64 : (i + 1) * 64]


def dot_nt(left, right):
    return lax.dot_general(left, right, (((1,), (1,)), ((), ())), preferred_element_type=F32)


def dot_tn(left, right):
    return lax.dot_general(left, right, (((0,), (0,)), ((), ())), preferred_element_type=F32)


def call(kernel, outs, cost, scratch=(), whole=0, after=0, stay=0):
    flops, nbytes = cost

    def body(*refs):
        n = len(refs) - len(outs) - len(scratch)
        kernel(*refs[: n - after], *refs[n:])

    def run(*args):
        plain = len(args) - whole - after
        kept = [
            pltpu.with_memory_space_constraint(arg, pltpu.HBM)
            for arg in args[plain : plain + whole + stay]
        ]
        return pl.pallas_call(
            body,
            out_shape=[(pltpu.HBM if o[2:] else jax.ShapeDtypeStruct)(*o[:2]) for o in outs],
            in_specs=[SMEM] + [VMEM] * (plain - 1) + [HBM] * (whole + stay) + [ANY] * (after - stay),
            out_specs=[HBM if o[2:] else VMEM for o in outs],
            scratch_shapes=list(scratch),
            cost_estimate=pl.CostEstimate(flops=flops, bytes_accessed=nbytes, transcendentals=0),
            compiler_params=pltpu.CompilerParams(vmem_limit_bytes=16 * 2**20),
        )(*args[:plain], *kept, *args[plain + whole + stay :])

    return run


def start_all(copies):
    for copy in copies:
        copy.start()
    return copies


def wait_all(copies):
    for copy in copies:
        copy.wait()


def pair_kernel(pos, other, rows_other, mine, rows_mine, gate, up, out, rows_out, acts_out, sems):
    row = pl.multiple_of(pos[2] * 32, 32)
    other_row = pl.multiple_of(32 - pos[2] * 32, 32)
    moves = [
        (mine, out.at[pl.ds(row, 32)]),
        (other, out.at[pl.ds(other_row, 32)]),
        (rows_mine, rows_out.at[pl.ds(row, 32)]),
        (rows_other, rows_out.at[pl.ds(other_row, 32)]),
        (gate, acts_out.at[pl.ds(0, 128)]),
        (up, acts_out.at[pl.ds(128, 128)]),
    ]
    wait_all(
        start_all([pltpu.make_async_copy(a, b, sems.at[i]) for i, (a, b) in enumerate(moves)])
    )


def rows_kernel(pos, *refs):
    for i, part in enumerate(refs[:4]):
        refs[4][i * 64 : (i + 1) * 64] = part[...]


def hidden_grad_kernel(pos, *refs):
    pieces, w_down, rows, (grads, keep, send, rows_out) = refs[:4], refs[4], refs[5:9], refs[9:]
    for j, piece in enumerate(pieces):
        to_local(pos, piece, grads, lambda k, j=j: ((pos[0] - k) & 3, (pos[1] - j) & 3))
    for start, width in COL_TILES:
        cols = slice(start, start + width)
        part = dot_nt(grads[...], w_down[cols, :])
        keep[:, cols] = part[:512]
        send[:, cols] = part[512:]
    for i, part in enumerate(rows):
        rows_out[i * 64 : (i + 1) * 64] = part[...]


def acts_kernel(pos, here, below, above, far_gate, far_up, out):
    row = 0
    for block in (here, below, far_gate, far_up, above):
        rows = block.shape[0]
        out[row : row + rows] = block[...]
        row += rows


def pair_sum_kernel(pos, keep, got, own, one, two, three):
    own[...] = keep[:128] + got[:128]
    for k, out in enumerate((one, two, three)):
        rows = slice(128 * (k + 1), 128 * (k + 2))
        out[...] = (keep[rows] + got[rows]).astype(BF)


def ring_sum_kernel(pos, own, one, two, three, out):
    total = own[...] + one[...].astype(F32) + two[...].astype(F32) + three[...].astype(F32)
    out[...] = total.astype(BF)


def down_kernel(pos, *refs):
    blocks, near, far, grads, out, act_out, slope_out, rows_out, hidden = refs[:2], *refs[2:]
    rows_out[:256] = near[...]
    rows_out[256:] = far[...]
    for i in range(8):
        rows = slice(i * 128, (i + 1) * 128)
        start = 256 * (i % 4)
        gate = blocks[i // 4][start : start + 128].astype(F32)
        up = blocks[i // 4][start + 128 : start + 256].astype(F32)
        sig = jax.nn.sigmoid(gate)
        act = gate * sig
        act_out[rows] = act
        slope_out[rows] = up * sig * (1.0 + gate * (1.0 - sig))
        hidden[rows] = (act * up).astype(BF)
    for start in range(0, DB, 256):
        cols = slice(start, start + 256)
        out[:, cols] = dot_tn(hidden[...], grads[:, cols]).astype(BF)


def sum_kernel(pos, parts, out):
    total = parts[0].astype(F32)
    for i in range(1, 32):
        total = total + parts[i].astype(F32)
    out[...] = total.astype(BF)


def input_grad_kernel(pos, *refs):
    hgs, (act, slope, w_gate, w_up, out, gate_out, up_out) = refs[:8], refs[8:15]
    gate_grad, up_grad, part, sems = refs[15:]
    for i in range(8):
        rows = slice(i * 128, (i + 1) * 128)
        hg = hgs[i][...].astype(F32)
        gate_grad[rows] = (hg * slope[rows]).astype(BF)
        up_grad[rows] = (hg * act[rows]).astype(BF)
    copies = start_all(
        [
            pltpu.make_async_copy(gate_grad, gate_out, sems.at[4]),
            pltpu.make_async_copy(up_grad, up_out, sems.at[5]),
        ]
    )
    zh, core = pos[3], pos[4]
    for n, start in enumerate(range(0, DB, 256)):
        cols = slice(start, start + 256)
        block = dot_nt(gate_grad[...], w_gate[cols, :]) + dot_nt(up_grad[...], w_up[cols, :])
        block = block.astype(BF)
        for i in range(8):
            bx = (zh + i % 4) & 3
            by = 2 * ((i // 4) ^ core)
            row = pl.multiple_of(bx * 256 + by * 64, 128)
            part[n, pl.ds(row, 128)] = block[i * 128 : (i + 1) * 128]
        copies += start_all([pltpu.make_async_copy(part.at[n], out.at[:, cols], sems.at[n])])
    wait_all(copies)


def weight_grad_kernel(pos, *refs):
    near, far, gate_grad, up_grad, out_gate, out_up, inputs = refs
    for first, rows in ((0, near), (8, far)):

        def place(i, first=first):
            i += first
            return (i >> 1 & 1 | i >> 2 & 2) ^ pos[0], (i & 1 | i >> 1 & 2) ^ pos[1]

        to_local(pos, rows, inputs, place)
    for start, width in COL_TILES:
        cols = slice(start, start + width)
        out_gate[:, cols] = dot_tn(inputs[...], gate_grad[:, cols]).astype(BF)
        out_up[:, cols] = dot_tn(inputs[...], up_grad[:, cols]).astype(BF)


MM = 2 * T * DB * FB
MB = 2**20
LONG = (12 * MM, 80 * MB)
SHORT = (0, 0)


def spread_core(mine):
    return list(mine) + [swap_core(p) for p in mine]


def gather_zh(block):
    got = [shift_zh(block, k) for k in (1, 2, 3)]
    return [block, got[2], got[1], got[0]]


def ring_zh(block):
    above, below = shift_zh(block, 1), shift_zh(block, 3)
    return [block, below, above, shift_zh(above[:128], 1), shift_zh(below[128:], 3)]


def per_device(inputs, out_grad, gate_pre, up_pre, w_gate, w_up, w_down):
    h, w = lax.axis_index("hid"), lax.axis_index("wid")
    pos = jnp.stack([h // 8, h // 2 % 4, h % 2, w // 2, w % 2]).astype(jnp.int32)

    block, near, acts = call(
        pair_kernel,
        [((64, DB), BF), ((64, DB), BF), ((256, FB), BF)],
        SHORT,
        [pltpu.SemaphoreType.DMA((6,))],
        whole=4,
    )(pos, swap_zl(out_grad), swap_zl(inputs), out_grad, inputs, gate_pre, up_pre)
    acts = ring_zh(acts)
    (block,) = call(rows_kernel, [((256, DB), BF)], (0, MB))(
        pos, block, *[shift_x(block, k) for k in (1, 2, 3)]
    )
    near = [near, swap_y(near, 1)]
    near += [swap_x(part, 1) for part in near]
    all_grads, keep, send, near = call(
        hidden_grad_kernel,
        [((T, DB), BF), ((512, FB), F32), ((512, FB), F32), ((256, DB), BF)],
        LONG,
        after=2,
    )(pos, block, *[shift_y(block, k) for k in (1, 2, 3)], w_down, *near, *acts[3:])
    far = swap_y(near, 2)
    (acts,) = call(acts_kernel, [((T, FB), BF)], SHORT, after=1)(pos, *acts, near)
    own, one, two, three = call(
        pair_sum_kernel, [((128, FB), F32)] + [((128, FB), BF)] * 3, LONG
    )(pos, keep, swap_core(send))
    got = [shift_zh(one, 1), shift_zh(two, 2), shift_zh(three, 3)]
    grad_down, act, slope, near = call(
        down_kernel,
        [((FB, DB), BF), ((T, FB), F32), ((T, FB), F32), ((512, DB), BF)],
        (MM, 16 * MB),
        [pltpu.VMEM((T, FB), BF)],
    )(pos, acts, swap_core(acts), near, far, all_grads)
    far = swap_x(near, 2)
    (hg,) = call(ring_sum_kernel, [((128, FB), BF)], LONG, after=1)(pos, own, *got, act)
    hgs = spread_core(gather_zh(hg))
    partial, gate_grad, up_grad = call(
        input_grad_kernel,
        [((T, DB), BF, HBM), ((T, FB), BF, HBM), ((T, FB), BF, HBM)],
        (2 * MM, 15 * MB),
        [
            pltpu.VMEM((T, FB), BF),
            pltpu.VMEM((T, FB), BF),
            pltpu.VMEM((4, T, 256), BF),
            pltpu.SemaphoreType.DMA((6,)),
        ],
        after=1,
    )(pos, *hgs, act, slope, w_gate, w_up, far)
    parts = lax.all_to_all(partial, "hid", split_axis=0, concat_axis=0, tiled=True)
    (grad_inputs,) = call(sum_kernel, [((32, DB), BF)], (MB, 2 * MB))(
        pos, parts.reshape(32, 32, DB)
    )
    grad_gate, grad_up = call(
        weight_grad_kernel,
        [((DB, FB), BF), ((DB, FB), BF)],
        (2 * MM, 10 * MB),
        [pltpu.VMEM((T, DB), BF)],
    )(pos, near, far, gate_grad, up_grad)
    return (grad_inputs, grad_gate, grad_up, grad_down)


def solution(mesh):
    in_specs = (
        P("hid", "wid"),
        P("hid", "wid"),
        P("wid", "hid"),
        P("wid", "hid"),
        P("wid", "hid"),
        P("wid", "hid"),
        P("hid", "wid"),
    )
    out_specs = (P("hid", "wid"), P("wid", "hid"), P("wid", "hid"), P("hid", "wid"))
    return jax.shard_map(
        per_device, mesh=mesh, in_specs=in_specs, out_specs=out_specs, check_vma=False
    )
```

```python
import functools

import jax
import jax.numpy as jnp
from jax import lax
from jax.experimental import pallas as pl
from jax.experimental.pallas import tpu as pltpu
from jax.sharding import PartitionSpec as P

BF = jnp.bfloat16
F32 = jnp.float32
T, DB, FB = 1024, 1024, 896
COL_TILES = ((0, 256), (256, 256), (512, 256), (768, 128))
VMEM = pl.BlockSpec(memory_space=pltpu.VMEM)
ANY = pl.BlockSpec(memory_space=pl.ANY)
HBM = pl.BlockSpec(memory_space=pltpu.HBM)
SMEM = pl.BlockSpec(memory_space=pltpu.SMEM)


def shift_x(value, step):
    return lax.ppermute(value, "hid", [(h, (h + 8 * step) % 32) for h in range(32)])


def shift_y(value, step):
    return lax.ppermute(
        value, "hid", [(h, h // 8 * 8 + (h % 8 + 2 * step) % 8) for h in range(32)]
    )


def swap_x(value, bit):
    return lax.ppermute(value, "hid", [(h, h ^ (8 * bit)) for h in range(32)])


def swap_y(value, bit):
    return lax.ppermute(value, "hid", [(h, h ^ (2 * bit)) for h in range(32)])


def swap_zl(value):
    return lax.ppermute(value, "hid", [(h, h ^ 1) for h in range(32)])


def shift_zh(value, step):
    return lax.ppermute(value, "wid", [(w, (w + 2 * step) % 8) for w in range(8)])


def swap_core(value):
    return lax.ppermute(value, "wid", [(w, w ^ 1) for w in range(8)])


def local_row(pos, bx, by):
    zh, core = pos[3], pos[4]
    return pl.multiple_of(
        ((by // 2) ^ core) * 512 + ((bx - zh) & 3) * 128 + (by & 1) * 64, 64
    )


def to_local(pos, rows, out, place):
    for i in range(rows.shape[0] // 64):
        out[pl.ds(local_row(pos, *place(i)), 64)] = rows[i * 64 : (i + 1) * 64]


def dot_nt(left, right):
    return lax.dot_general(left, right, (((1,), (1,)), ((), ())), preferred_element_type=F32)


def dot_tn(left, right):
    return lax.dot_general(left, right, (((0,), (0,)), ((), ())), preferred_element_type=F32)


def call(kernel, outs, cost, scratch=(), whole=0, after=0, stay=0):
    flops, nbytes = cost

    def body(*refs):
        n = len(refs) - len(outs) - len(scratch)
        kernel(*refs[: n - after], *refs[n:])

    def run(*args):
        plain = len(args) - whole - after
        kept = [
            pltpu.with_memory_space_constraint(arg, pltpu.HBM)
            for arg in args[plain : plain + whole + stay]
        ]
        return pl.pallas_call(
            body,
            out_shape=[(pltpu.HBM if o[2:] else jax.ShapeDtypeStruct)(*o[:2]) for o in outs],
            in_specs=[SMEM] + [VMEM] * (plain - 1) + [HBM] * (whole + stay) + [ANY] * (after - stay),
            out_specs=[HBM if o[2:] else VMEM for o in outs],
            scratch_shapes=list(scratch),
            cost_estimate=pl.CostEstimate(flops=flops, bytes_accessed=nbytes, transcendentals=0),
            compiler_params=pltpu.CompilerParams(vmem_limit_bytes=16 * 2**20),
        )(*args[:plain], *kept, *args[plain + whole + stay :])

    return run


def start_all(copies):
    for copy in copies:
        copy.start()
    return copies


def wait_all(copies):
    for copy in copies:
        copy.wait()


def pair_kernel(pos, other, rows_other, mine, rows_mine, gate, up, out, rows_out, acts_out, sems):
    row = pl.multiple_of(pos[2] * 32, 32)
    other_row = pl.multiple_of(32 - pos[2] * 32, 32)
    moves = [
        (mine, out.at[pl.ds(row, 32)]),
        (other, out.at[pl.ds(other_row, 32)]),
        (rows_mine, rows_out.at[pl.ds(row, 32)]),
        (rows_other, rows_out.at[pl.ds(other_row, 32)]),
        (gate, acts_out.at[pl.ds(0, 128)]),
        (up, acts_out.at[pl.ds(128, 128)]),
    ]
    wait_all(
        start_all([pltpu.make_async_copy(a, b, sems.at[i]) for i, (a, b) in enumerate(moves)])
    )


def rows_kernel(pos, *refs):
    for i, part in enumerate(refs[:4]):
        refs[4][i * 64 : (i + 1) * 64] = part[...]


def hidden_grad(grads, w_down, out):
    for start, width in COL_TILES:
        cols = slice(start, start + width)
        out[:, cols] = dot_nt(grads[...], w_down[cols, :])


def send_kernel(pos, *refs):
    pieces, w_down, rows, (own, other, send, rows_out, local) = refs[:4], refs[4], refs[5:9], refs[9:]
    for j, piece in enumerate(pieces):
        to_local(pos, piece, local, lambda k, j=j: ((pos[0] - k) & 3, (pos[1] - j) & 3))
    own[...] = local[:512]
    other[...] = local[512:]
    hidden_grad(other, w_down, send)
    for i, part in enumerate(rows):
        rows_out[i * 64 : (i + 1) * 64] = part[...]


def keep_kernel(pos, own, w_down, keep):
    hidden_grad(own, w_down, keep)


def acts_kernel(pos, here, below, above, far_gate, far_up, out):
    row = 0
    for block in (here, below, far_gate, far_up, above):
        rows = block.shape[0]
        out[row : row + rows] = block[...]
        row += rows


def pair_sum_kernel(pos, keep, got, own, one, two, three):
    own[...] = keep[:128] + got[:128]
    for k, out in enumerate((one, two, three)):
        rows = slice(128 * (k + 1), 128 * (k + 2))
        out[...] = (keep[rows] + got[rows]).astype(BF)


def ring_sum_kernel(pos, own, one, two, three, out):
    total = own[...] + one[...].astype(F32) + two[...].astype(F32) + three[...].astype(F32)
    out[...] = total.astype(BF)


def down_kernel(pos, *refs):
    blocks, near, far, own, other, out, act_out, slope_out, rows_out, hidden = refs[:2], *refs[2:]
    rows_out[:256] = near[...]
    rows_out[256:] = far[...]
    for i in range(8):
        rows = slice(i * 128, (i + 1) * 128)
        start = 256 * (i % 4)
        gate = blocks[i // 4][start : start + 128].astype(F32)
        up = blocks[i // 4][start + 128 : start + 256].astype(F32)
        sig = jax.nn.sigmoid(gate)
        act = gate * sig
        act_out[rows] = act
        slope_out[rows] = up * sig * (1.0 + gate * (1.0 - sig))
        hidden[rows] = (act * up).astype(BF)
    for start in range(0, DB, 256):
        cols = slice(start, start + 256)
        total = dot_tn(hidden[:512], own[:, cols]) + dot_tn(hidden[512:], other[:, cols])
        out[:, cols] = total.astype(BF)


def sum_kernel(pos, parts, out):
    total = parts[0].astype(F32)
    for i in range(1, 32):
        total = total + parts[i].astype(F32)
    out[...] = total.astype(BF)


def input_grad_kernel(pos, *refs):
    hgs, (act, slope, w_gate, w_up, out, gate_out, up_out) = refs[:8], refs[8:15]
    gate_grad, up_grad, part, sems = refs[15:]
    for i in range(8):
        rows = slice(i * 128, (i + 1) * 128)
        hg = hgs[i][...].astype(F32)
        gate_grad[rows] = (hg * slope[rows]).astype(BF)
        up_grad[rows] = (hg * act[rows]).astype(BF)
    copies = start_all(
        [
            pltpu.make_async_copy(gate_grad, gate_out, sems.at[4]),
            pltpu.make_async_copy(up_grad, up_out, sems.at[5]),
        ]
    )
    zh, core = pos[3], pos[4]
    for n, start in enumerate(range(0, DB, 256)):
        cols = slice(start, start + 256)
        block = dot_nt(gate_grad[...], w_gate[cols, :]) + dot_nt(up_grad[...], w_up[cols, :])
        block = block.astype(BF)
        for i in range(8):
            bx = (zh + i % 4) & 3
            by = 2 * ((i // 4) ^ core)
            row = pl.multiple_of(bx * 256 + by * 64, 128)
            part[n, pl.ds(row, 128)] = block[i * 128 : (i + 1) * 128]
        copies += start_all([pltpu.make_async_copy(part.at[n], out.at[:, cols], sems.at[n])])
    wait_all(copies)


def weight_grad_kernel(pos, *refs):
    near, far, gate_grad, up_grad, out_gate, out_up, inputs = refs
    for first, rows in ((0, near), (8, far)):

        def place(i, first=first):
            i += first
            return (i >> 1 & 1 | i >> 2 & 2) ^ pos[0], (i & 1 | i >> 1 & 2) ^ pos[1]

        to_local(pos, rows, inputs, place)
    for start, width in COL_TILES:
        cols = slice(start, start + width)
        out_gate[:, cols] = dot_tn(inputs[...], gate_grad[:, cols]).astype(BF)
        out_up[:, cols] = dot_tn(inputs[...], up_grad[:, cols]).astype(BF)


MM = 2 * T * DB * FB
MB = 2**20
LONG = (12 * MM, 80 * MB)
SHORT = (0, 0)


def spread_core(mine):
    return list(mine) + [swap_core(p) for p in mine]


def gather_zh(block):
    got = [shift_zh(block, k) for k in (1, 2, 3)]
    return [block, got[2], got[1], got[0]]


def ring_zh(block):
    above, below = shift_zh(block, 1), shift_zh(block, 3)
    return [block, below, above, shift_zh(above[:128], 1), shift_zh(below[128:], 3)]


def per_device(inputs, out_grad, gate_pre, up_pre, w_gate, w_up, w_down):
    h, w = lax.axis_index("hid"), lax.axis_index("wid")
    pos = jnp.stack([h // 8, h // 2 % 4, h % 2, w // 2, w % 2]).astype(jnp.int32)

    block, near, acts = call(
        pair_kernel,
        [((64, DB), BF), ((64, DB), BF), ((256, FB), BF)],
        SHORT,
        [pltpu.SemaphoreType.DMA((6,))],
        whole=4,
    )(pos, swap_zl(out_grad), swap_zl(inputs), out_grad, inputs, gate_pre, up_pre)
    acts = ring_zh(acts)
    (block,) = call(rows_kernel, [((256, DB), BF)], (0, MB))(
        pos, block, *[shift_x(block, k) for k in (1, 2, 3)]
    )
    near = [near, swap_y(near, 1)]
    near += [swap_x(part, 1) for part in near]
    own_grads, other_grads, send, near = call(
        send_kernel,
        [((512, DB), BF), ((512, DB), BF), ((512, FB), F32), ((256, DB), BF)],
        LONG,
        [pltpu.VMEM((T, DB), BF)],
        after=2,
    )(pos, block, *[shift_y(block, k) for k in (1, 2, 3)], w_down, *near, *acts[3:])
    (keep,) = call(keep_kernel, [((512, FB), F32)], (MM // 2, 4 * MB))(pos, own_grads, w_down)
    far = swap_y(near, 2)
    (acts,) = call(acts_kernel, [((T, FB), BF)], SHORT, after=1)(pos, *acts, near)
    own, one, two, three = call(
        pair_sum_kernel, [((128, FB), F32)] + [((128, FB), BF)] * 3, LONG
    )(pos, keep, swap_core(send))
    got = [shift_zh(one, 1), shift_zh(two, 2), shift_zh(three, 3)]
    grad_down, act, slope, near = call(
        down_kernel,
        [((FB, DB), BF), ((T, FB), F32), ((T, FB), F32), ((512, DB), BF)],
        (MM, 16 * MB),
        [pltpu.VMEM((T, FB), BF)],
    )(pos, acts, swap_core(acts), near, far, own_grads, other_grads)
    far = swap_x(near, 2)
    (hg,) = call(ring_sum_kernel, [((128, FB), BF)], LONG, after=1)(pos, own, *got, act)
    hgs = spread_core(gather_zh(hg))
    partial, gate_grad, up_grad = call(
        input_grad_kernel,
        [((T, DB), BF, HBM), ((T, FB), BF, HBM), ((T, FB), BF, HBM)],
        (2 * MM, 15 * MB),
        [
            pltpu.VMEM((T, FB), BF),
            pltpu.VMEM((T, FB), BF),
            pltpu.VMEM((4, T, 256), BF),
            pltpu.SemaphoreType.DMA((6,)),
        ],
        after=1,
    )(pos, *hgs, act, slope, w_gate, w_up, far)
    parts = lax.all_to_all(partial, "hid", split_axis=0, concat_axis=0, tiled=True)
    (grad_inputs,) = call(sum_kernel, [((32, DB), BF)], (MB, 2 * MB))(
        pos, parts.reshape(32, 32, DB)
    )
    grad_gate, grad_up = call(
        weight_grad_kernel,
        [((DB, FB), BF), ((DB, FB), BF)],
        (2 * MM, 10 * MB),
        [pltpu.VMEM((T, DB), BF)],
    )(pos, near, far, gate_grad, up_grad)
    return (grad_inputs, grad_gate, grad_up, grad_down)


def solution(mesh):
    in_specs = (
        P("hid", "wid"),
        P("hid", "wid"),
        P("wid", "hid"),
        P("wid", "hid"),
        P("wid", "hid"),
        P("wid", "hid"),
        P("hid", "wid"),
    )
    out_specs = (P("hid", "wid"), P("wid", "hid"), P("wid", "hid"), P("hid", "wid"))
    return jax.shard_map(
        per_device, mesh=mesh, in_specs=in_specs, out_specs=out_specs, check_vma=False
    )
```

```python
import functools

import jax
import jax.numpy as jnp
from jax import lax
from jax.experimental import pallas as pl
from jax.experimental.pallas import tpu as pltpu
from jax.sharding import PartitionSpec as P

BF = jnp.bfloat16
F32 = jnp.float32
T, DB, FB = 1024, 1024, 896
COL_TILES = ((0, 256), (256, 256), (512, 256), (768, 128))
VMEM = pl.BlockSpec(memory_space=pltpu.VMEM)
ANY = pl.BlockSpec(memory_space=pl.ANY)
HBM = pl.BlockSpec(memory_space=pltpu.HBM)
SMEM = pl.BlockSpec(memory_space=pltpu.SMEM)


def shift_x(value, step):
    return lax.ppermute(value, "hid", [(h, (h + 8 * step) % 32) for h in range(32)])


def shift_y(value, step):
    return lax.ppermute(
        value, "hid", [(h, h // 8 * 8 + (h % 8 + 2 * step) % 8) for h in range(32)]
    )


def swap_x(value, bit):
    return lax.ppermute(value, "hid", [(h, h ^ (8 * bit)) for h in range(32)])


def swap_y(value, bit):
    return lax.ppermute(value, "hid", [(h, h ^ (2 * bit)) for h in range(32)])


def swap_zl(value):
    return lax.ppermute(value, "hid", [(h, h ^ 1) for h in range(32)])


def shift_zh(value, step):
    return lax.ppermute(value, "wid", [(w, (w + 2 * step) % 8) for w in range(8)])


def swap_core(value):
    return lax.ppermute(value, "wid", [(w, w ^ 1) for w in range(8)])


def local_row(pos, bx, by):
    zh, core = pos[3], pos[4]
    return pl.multiple_of(
        ((by // 2) ^ core) * 512 + ((bx - zh) & 3) * 128 + (by & 1) * 64, 64
    )


def to_local(pos, rows, out, place):
    for i in range(rows.shape[0] // 64):
        out[pl.ds(local_row(pos, *place(i)), 64)] = rows[i * 64 : (i + 1) * 64]


def dot_nt(left, right):
    return lax.dot_general(left, right, (((1,), (1,)), ((), ())), preferred_element_type=F32)


def dot_tn(left, right):
    return lax.dot_general(left, right, (((0,), (0,)), ((), ())), preferred_element_type=F32)


def call(kernel, outs, cost, scratch=(), whole=0, after=0, stay=0):
    flops, nbytes = cost

    def body(*refs):
        n = len(refs) - len(outs) - len(scratch)
        kernel(*refs[: n - after], *refs[n:])

    def run(*args):
        plain = len(args) - whole - after
        kept = [
            pltpu.with_memory_space_constraint(arg, pltpu.HBM)
            for arg in args[plain : plain + whole + stay]
        ]
        return pl.pallas_call(
            body,
            out_shape=[(pltpu.HBM if o[2:] else jax.ShapeDtypeStruct)(*o[:2]) for o in outs],
            in_specs=[SMEM] + [VMEM] * (plain - 1) + [HBM] * (whole + stay) + [ANY] * (after - stay),
            out_specs=[HBM if o[2:] else VMEM for o in outs],
            scratch_shapes=list(scratch),
            cost_estimate=pl.CostEstimate(flops=flops, bytes_accessed=nbytes, transcendentals=0),
            compiler_params=pltpu.CompilerParams(vmem_limit_bytes=16 * 2**20),
        )(*args[:plain], *kept, *args[plain + whole + stay :])

    return run


def start_all(copies):
    for copy in copies:
        copy.start()
    return copies


def wait_all(copies):
    for copy in copies:
        copy.wait()


def pair_kernel(pos, other, rows_other, mine, rows_mine, gate, up, out, rows_out, acts_out, sems):
    row = pl.multiple_of(pos[2] * 32, 32)
    other_row = pl.multiple_of(32 - pos[2] * 32, 32)
    moves = [
        (mine, out.at[pl.ds(row, 32)]),
        (other, out.at[pl.ds(other_row, 32)]),
        (rows_mine, rows_out.at[pl.ds(row, 32)]),
        (rows_other, rows_out.at[pl.ds(other_row, 32)]),
        (gate, acts_out.at[pl.ds(0, 128)]),
        (up, acts_out.at[pl.ds(128, 128)]),
    ]
    wait_all(
        start_all([pltpu.make_async_copy(a, b, sems.at[i]) for i, (a, b) in enumerate(moves)])
    )


def rows_kernel(pos, *refs):
    for i, part in enumerate(refs[:4]):
        refs[4][i * 64 : (i + 1) * 64] = part[...]


def hidden_grad_kernel(pos, *refs):
    pieces, w_down, rows, (grads, keep, send, rows_out) = refs[:4], refs[4], refs[5:9], refs[9:]
    for j, piece in enumerate(pieces):
        to_local(pos, piece, grads, lambda k, j=j: ((pos[0] - k) & 3, (pos[1] - j) & 3))
    for start, width in COL_TILES:
        cols = slice(start, start + width)
        part = dot_nt(grads[...], w_down[cols, :])
        keep[:, cols] = part[:512]
        send[:, cols] = part[512:]
    for i, part in enumerate(rows):
        rows_out[i * 64 : (i + 1) * 64] = part[...]


def acts_kernel(pos, here, below, above, far_gate, far_up, out):
    row = 0
    for block in (here, below, far_gate, far_up, above):
        rows = block.shape[0]
        out[row : row + rows] = block[...]
        row += rows


def pair_sum_kernel(pos, keep, got, own, one, two, three):
    own[...] = keep[:128] + got[:128]
    for k, out in enumerate((one, two, three)):
        rows = slice(128 * (k + 1), 128 * (k + 2))
        out[...] = (keep[rows] + got[rows]).astype(BF)


def ring_sum_kernel(pos, own, one, two, three, out):
    total = own[...] + one[...].astype(F32) + two[...].astype(F32) + three[...].astype(F32)
    out[...] = total.astype(BF)


def down_kernel(pos, *refs):
    blocks, near, far, grads, out, act_out, slope_out, rows_out, hidden = refs[:2], *refs[2:]
    rows_out[:256] = near[...]
    rows_out[256:] = far[...]
    for i in range(8):
        rows = slice(i * 128, (i + 1) * 128)
        start = 256 * (i % 4)
        gate = blocks[i // 4][start : start + 128].astype(F32)
        up = blocks[i // 4][start + 128 : start + 256].astype(F32)
        sig = jax.nn.sigmoid(gate)
        act = gate * sig
        act_out[rows] = act
        slope_out[rows] = up * sig * (1.0 + gate * (1.0 - sig))
        hidden[rows] = (act * up).astype(BF)
    for start in range(0, DB, 256):
        cols = slice(start, start + 256)
        out[:, cols] = dot_tn(hidden[...], grads[:, cols]).astype(BF)


def sum_kernel(pos, parts, out):
    for start in range(0, DB, 256):
        cols = slice(start, start + 256)
        even, odd = parts[0, :, cols].astype(F32), parts[1, :, cols].astype(F32)
        for i in range(2, 32, 2):
            even = even + parts[i, :, cols].astype(F32)
            odd = odd + parts[i + 1, :, cols].astype(F32)
        out[:, cols] = (even + odd).astype(BF)


def input_grad_kernel(pos, *refs):
    hgs, (act, slope, w_gate, w_up, out, gate_out, up_out) = refs[:8], refs[8:15]
    gate_grad, up_grad, part, sems = refs[15:]
    for i in range(8):
        rows = slice(i * 128, (i + 1) * 128)
        hg = hgs[i][...].astype(F32)
        gate_grad[rows] = (hg * slope[rows]).astype(BF)
        up_grad[rows] = (hg * act[rows]).astype(BF)
    copies = start_all(
        [
            pltpu.make_async_copy(gate_grad, gate_out, sems.at[4]),
            pltpu.make_async_copy(up_grad, up_out, sems.at[5]),
        ]
    )
    zh, core = pos[3], pos[4]
    for n, start in enumerate(range(0, DB, 256)):
        cols = slice(start, start + 256)
        block = dot_nt(gate_grad[...], w_gate[cols, :]) + dot_nt(up_grad[...], w_up[cols, :])
        block = block.astype(BF)
        for i in range(8):
            bx = (zh + i % 4) & 3
            by = 2 * ((i // 4) ^ core)
            row = pl.multiple_of(bx * 256 + by * 64, 128)
            part[n, pl.ds(row, 128)] = block[i * 128 : (i + 1) * 128]
        copies += start_all([pltpu.make_async_copy(part.at[n], out.at[:, cols], sems.at[n])])
    wait_all(copies)


def weight_grad_kernel(pos, *refs):
    near, far, gate_grad, up_grad, out_gate, out_up, inputs = refs
    for first, rows in ((0, near), (8, far)):

        def place(i, first=first):
            i += first
            return (i >> 1 & 1 | i >> 2 & 2) ^ pos[0], (i & 1 | i >> 1 & 2) ^ pos[1]

        to_local(pos, rows, inputs, place)
    for start, width in COL_TILES:
        cols = slice(start, start + width)
        out_gate[:, cols] = dot_tn(inputs[...], gate_grad[:, cols]).astype(BF)
        out_up[:, cols] = dot_tn(inputs[...], up_grad[:, cols]).astype(BF)


MM = 2 * T * DB * FB
MB = 2**20
LONG = (12 * MM, 80 * MB)
SHORT = (0, 0)


def spread_core(mine):
    return list(mine) + [swap_core(p) for p in mine]


def gather_zh(block):
    got = [shift_zh(block, k) for k in (1, 2, 3)]
    return [block, got[2], got[1], got[0]]


def ring_zh(block):
    above, below = shift_zh(block, 1), shift_zh(block, 3)
    return [block, below, above, shift_zh(above[:128], 1), shift_zh(below[128:], 3)]


def per_device(inputs, out_grad, gate_pre, up_pre, w_gate, w_up, w_down):
    h, w = lax.axis_index("hid"), lax.axis_index("wid")
    pos = jnp.stack([h // 8, h // 2 % 4, h % 2, w // 2, w % 2]).astype(jnp.int32)

    block, near, acts = call(
        pair_kernel,
        [((64, DB), BF), ((64, DB), BF), ((256, FB), BF)],
        SHORT,
        [pltpu.SemaphoreType.DMA((6,))],
        whole=4,
    )(pos, swap_zl(out_grad), swap_zl(inputs), out_grad, inputs, gate_pre, up_pre)
    acts = ring_zh(acts)
    (block,) = call(rows_kernel, [((256, DB), BF)], (0, MB))(
        pos, block, *[shift_x(block, k) for k in (1, 2, 3)]
    )
    near = [near, swap_y(near, 1)]
    near += [swap_x(part, 1) for part in near]
    all_grads, keep, send, near = call(
        hidden_grad_kernel,
        [((T, DB), BF), ((512, FB), F32), ((512, FB), F32), ((256, DB), BF)],
        LONG,
        after=2,
    )(pos, block, *[shift_y(block, k) for k in (1, 2, 3)], w_down, *near, *acts[3:])
    far = swap_y(near, 2)
    (acts,) = call(acts_kernel, [((T, FB), BF)], SHORT, after=1)(pos, *acts, near)
    own, one, two, three = call(
        pair_sum_kernel, [((128, FB), F32)] + [((128, FB), BF)] * 3, LONG
    )(pos, keep, swap_core(send))
    got = [shift_zh(one, 1), shift_zh(two, 2), shift_zh(three, 3)]
    grad_down, act, slope, near = call(
        down_kernel,
        [((FB, DB), BF), ((T, FB), F32), ((T, FB), F32), ((512, DB), BF)],
        (MM, 16 * MB),
        [pltpu.VMEM((T, FB), BF)],
    )(pos, acts, swap_core(acts), near, far, all_grads)
    far = swap_x(near, 2)
    (hg,) = call(ring_sum_kernel, [((128, FB), BF)], LONG, after=1)(pos, own, *got, act)
    hgs = spread_core(gather_zh(hg))
    partial, gate_grad, up_grad = call(
        input_grad_kernel,
        [((T, DB), BF, HBM), ((T, FB), BF, HBM), ((T, FB), BF, HBM)],
        (2 * MM, 15 * MB),
        [
            pltpu.VMEM((T, FB), BF),
            pltpu.VMEM((T, FB), BF),
            pltpu.VMEM((4, T, 256), BF),
            pltpu.SemaphoreType.DMA((6,)),
        ],
        after=1,
    )(pos, *hgs, act, slope, w_gate, w_up, far)
    parts = lax.all_to_all(partial, "hid", split_axis=0, concat_axis=0, tiled=True)
    (grad_inputs,) = call(sum_kernel, [((32, DB), BF)], (MB, 2 * MB))(
        pos, parts.reshape(32, 32, DB)
    )
    grad_gate, grad_up = call(
        weight_grad_kernel,
        [((DB, FB), BF), ((DB, FB), BF)],
        (2 * MM, 10 * MB),
        [pltpu.VMEM((T, DB), BF)],
    )(pos, near, far, gate_grad, up_grad)
    return (grad_inputs, grad_gate, grad_up, grad_down)


def solution(mesh):
    in_specs = (
        P("hid", "wid"),
        P("hid", "wid"),
        P("wid", "hid"),
        P("wid", "hid"),
        P("wid", "hid"),
        P("wid", "hid"),
        P("hid", "wid"),
    )
    out_specs = (P("hid", "wid"), P("wid", "hid"), P("wid", "hid"), P("hid", "wid"))
    return jax.shard_map(
        per_device, mesh=mesh, in_specs=in_specs, out_specs=out_specs, check_vma=False
    )
```
